32 devices in a mesh: query: 2 (over y), tok: 2 (over core), row: 4 (over z), col: 2 (over x).
Axes of the slice: x: 2, y: 2, z: 4, core: 2. Of those that a mesh axis runs over, the one named last changes fastest.
Arguments:
- activations: bfloat16 [128, 2560], P(('query', 'row'), ('tok', 'col')), parts along dimension 0, may hold values from -6 to 6
- out_grads: bfloat16 [128, 6912], P(('query', 'tok', 'col'), 'row'), parts along dimension 0, may hold values from -6 to 6
- left_basis: float32 [2560, 2560], P(('tok', 'col'), 'row'), may hold values from -0.125 to 0.125
- right_basis: float32 [6912, 6912], P('row', ('tok', 'col')), may hold values from -0.078125 to 0.078125
- spectrum: float32 [2560, 6912], P('row', ('tok', 'col')), may hold values from 0.005 to 0.1
Outputs:
- preconditioned: float32 [5120, 6912], P(('query', 'tok', 'col'), 'row'), parts along dimension 0
The draws below stay inside these ranges and needn't reach their ends.
There are 2 independent parts, one for each index of `query`. The reference program is written for one: setup_inputs(seed, part) draws one part's arguments, and reference() takes and returns one part's arrays. A program takes and returns all parts, laid end to end along the dimension named above; an argument that names none is the same for every part. Nothing has to cross between parts.
All inputs are finite; a program needn't handle non-finite values.
Results may differ from the reference program's by a relative error of at most 0.003.
Values may be sent and summed in bfloat16 or wider, within the bound.
A program may use at most 128 MiB of HBM per device.

```python
import math
import jax
import jax.numpy as jnp
from jax import lax

D = 2560
FF = 6912
TOKENS = 64


def block_levels(key, extent, shards, smallest, largest):
    loudness = 1.0
    for position, blocks in shards:
        steps = jax.random.uniform(jax.random.fold_in(jax.random.fold_in(key, 6), position), (blocks,), jnp.float32, smallest / len(shards), largest / len(shards))
        loudness = loudness * jnp.repeat(jnp.exp(steps), extent[position] // blocks).reshape((-1,) + (1,) * (len(extent) - 1 - position))
    return loudness


def gaussian(key, shape, scale, bound, split=(), kind=jnp.bfloat16):
    factor_of = block_levels(key, shape, split, -0.22, 0.18) if split else 1.0
    entries = jax.random.normal(key, shape, jnp.float32) * scale * factor_of
    return jnp.minimum(jnp.maximum(entries, -bound), bound).astype(kind)


def setup_inputs(seed: int = 0, part: int = 0) -> dict:
    keys = jax.random.split(jax.random.key(seed), 6)
    part_keys = jax.random.split(jax.random.fold_in(keys[5], part), 6)
    return {
        "activations": gaussian(part_keys[0], (TOKENS, D), 1.0, 6.0, ((0, 4), (1, 4))),
        "out_grads": gaussian(part_keys[1], (TOKENS, FF), 1.0, 6.0, ((0, 4), (1, 4))),
        "left_basis": gaussian(keys[2], (D, D), D ** -0.5, 0.125, ((0, 4), (1, 4)), jnp.float32),
        "right_basis": gaussian(keys[3], (FF, FF), FF ** -0.5, 0.078125, ((0, 4), (1, 4)), jnp.float32),
        "spectrum": jnp.clip(jnp.exp(math.log(0.1) - 2.9957323 * jax.random.uniform(keys[4], (D, FF), jnp.float32) ** block_levels(keys[4], (D, FF), ((0, 4), (1, 4)), -0.2, 0.2)), 0.005, 0.1),
    }


DAMPING = 0.002


def product(left, right):
    return jnp.dot(left, right, precision=lax.Precision.HIGHEST, preferred_element_type=jnp.float32)


def reference(activations, out_grads, left_basis, right_basis, spectrum):
    rotated_acts = product(activations.astype(jnp.float32), left_basis)
    rotated_grads = product(out_grads.astype(jnp.float32), right_basis)
    rotated = product(rotated_acts.T, rotated_grads) / TOKENS
    scaled = (rotated / (spectrum + DAMPING)).astype(jnp.bfloat16)
    back = product(scaled.astype(jnp.float32), right_basis.T).astype(jnp.bfloat16)
    return product(left_basis, back.astype(jnp.float32))
```

```python
import jax
import jax.numpy as jnp
from jax import lax
from jax.sharding import PartitionSpec as P

DAMPING = 0.002
F32, BF16, F16 = jnp.float32, jnp.bfloat16, jnp.float16


def shift(x, axis, n, s):
    return lax.ppermute(x, axis, [(i, (i + s) % n) for i in range(n)])


def gather(x, axis, n):
    me = lax.axis_index(axis)
    if n == 2:
        other = shift(x, axis, n, 1)
        return jnp.stack([jnp.where(me == 0, x, other), jnp.where(me == 0, other, x)])
    out = jnp.zeros((n,) + x.shape, x.dtype)
    out = lax.dynamic_update_index_in_dim(out, x, me, 0)
    for s in range(1, n):
        out = lax.dynamic_update_index_in_dim(out, shift(x, axis, n, s), (me - s) % n, 0)
    return out


def exchange_sum(x, axis, n, sent=F32):
    total = x
    for s in range(1, n):
        total = total + shift(x.astype(sent), axis, n, s).astype(F32)
    return total


def scatter_sum(x, axis, n):
    me = lax.axis_index(axis)
    total = lax.dynamic_index_in_dim(x, me, 0, keepdims=False)
    for s in range(1, n):
        part = lax.dynamic_index_in_dim(x, (me + s) % n, 0, keepdims=False)
        total = total + shift(part, axis, n, s)
    return total


def narrow(left, right, dims):
    return lax.dot_general(left, right, (dims, ((), ())), preferred_element_type=F32)


def wide(left, right):
    return jnp.dot(left, right, precision=lax.Precision.HIGH, preferred_element_type=F32)


def halves(x):
    high = lax.reduce_precision(x, 8, 7)
    return high.astype(BF16), (x - high).astype(BF16)


def shards(sizes, activations, out_grads, left_basis, right_basis, spectrum):
    nq, nt, nr, nc = (sizes[a] for a in ("query", "tok", "row", "col"))
    query, row, tok = (lax.axis_index(a) for a in ("query", "row", "tok"))
    block, width = spectrum.shape

    share = block // nq
    ring = lax.dynamic_slice_in_dim(spectrum, query * share, share, 0).astype(F16)
    spectra = [spectrum]
    for _ in range(1, nr):
        ring = shift(ring, "row", nr, 1)
        spectra.append(gather(ring, "query", nq).reshape(block, width))

    grads = gather(gather(out_grads, "col", nc), "tok", nt).reshape(-1, out_grads.shape[1])
    grads = wide(grads.astype(F32), right_basis)
    tokens = grads.shape[0]
    grads = scatter_sum(grads.reshape(nr, tokens // nr, width), "row", nr)
    grads = gather(grads, "row", nr).reshape(tokens, width) * (1.0 / tokens)
    high, low = halves(grads)
    grads = jnp.concatenate([high, low, high], 0)

    acts = gather(activations, "row", nr).reshape(tokens, -1)
    acts = wide(acts.astype(F32), left_basis)
    acts = exchange_sum(exchange_sum(acts, "tok", nt), "col", nc)
    acts = [acts] + [shift(acts, "row", nr, s) for s in range(1, nr)]

    lefts = [left_basis.astype(BF16)]
    for _ in range(1, nr):
        lefts.append(shift(lefts[-1], "row", nr, 1))

    right = right_basis.astype(BF16)
    half = block // nt
    out = None
    for s in range(nr):
        high, low = halves(acts[s])
        rotated = narrow(jnp.concatenate([high, high, low], 0), grads, ((0,), (0,)))
        scaled = (rotated / (spectra[s].astype(F32) + DAMPING)).astype(BF16)
        part = narrow(scaled, right, ((1,), (1,))).reshape(nt, half, -1)
        back = scatter_sum(part, "tok", nt)
        back = exchange_sum(back, "col", nc, BF16).astype(BF16)
        back = gather(back, "tok", nt).reshape(block, -1)
        term = narrow(lefts[s], back, ((1,), (0,)))
        out = term if out is None else out + term
    return out


def solution(mesh):
    sizes = dict(mesh.shape)
    return jax.shard_map(
        lambda *args: shards(sizes, *args),
        mesh=mesh,
        in_specs=(
            P(("query", "row"), ("tok", "col")),
            P(("query", "tok", "col"), "row"),
            P(("tok", "col"), "row"),
            P("row", ("tok", "col")),
            P("row", ("tok", "col")),
        ),
        out_specs=P(("query", "tok", "col"), "row"),
        check_vma=False,
    )
```

```python
import jax
import jax.numpy as jnp
from jax import lax
from jax.sharding import PartitionSpec as P

DAMPING = 0.002
F32, BF16, F16 = jnp.float32, jnp.bfloat16, jnp.float16


def shift(x, axis, n, s):
    return lax.ppermute(x, axis, [(i, (i + s) % n) for i in range(n)])


def gather(x, axis, n):
    me = lax.axis_index(axis)
    if n == 2:
        other = shift(x, axis, n, 1)
        return jnp.stack([jnp.where(me == 0, x, other), jnp.where(me == 0, other, x)])
    out = jnp.zeros((n,) + x.shape, x.dtype)
    out = lax.dynamic_update_index_in_dim(out, x, me, 0)
    for s in range(1, n):
        out = lax.dynamic_update_index_in_dim(out, shift(x, axis, n, s), (me - s) % n, 0)
    return out


def exchange_sum(x, axis, n, sent=F32):
    total = x
    for s in range(1, n):
        total = total + shift(x.astype(sent), axis, n, s).astype(F32)
    return total


def scatter_sum(x, axis, n):
    me = lax.axis_index(axis)
    total = lax.dynamic_index_in_dim(x, me, 0, keepdims=False)
    for s in range(1, n):
        part = lax.dynamic_index_in_dim(x, (me + s) % n, 0, keepdims=False)
        total = total + shift(part, axis, n, s)
    return total


def narrow(left, right, dims):
    return lax.dot_general(left, right, (dims, ((), ())), preferred_element_type=F32)


def wide(left, right):
    return jnp.dot(left, right, precision=lax.Precision.HIGH, preferred_element_type=F32)


def halves(x):
    high = lax.reduce_precision(x, 8, 7)
    return high.astype(BF16), (x - high).astype(BF16)


def shards(sizes, activations, out_grads, left_basis, right_basis, spectrum):
    nq, nt, nr, nc = (sizes[a] for a in ("query", "tok", "row", "col"))
    query, row, tok = (lax.axis_index(a) for a in ("query", "row", "tok"))
    block, width = spectrum.shape

    def share(x):
        size = x.shape[0] // nq
        return lax.dynamic_slice_in_dim(x, query * size, size, 0)

    def joined(piece):
        return gather(piece, "query", nq).reshape((-1,) + piece.shape[1:])

    spectra = [spectrum]
    ring = share(spectrum).astype(F16)
    if nr > 1:
        ring = shift(ring, "row", nr, 1)
        spectra.append(joined(ring))

    acts = gather(activations, "row", nr).reshape(-1, activations.shape[1])
    tokens = acts.shape[0]
    acts = wide(acts.astype(F32), left_basis)

    grads = gather(gather(out_grads, "col", nc), "tok", nt).reshape(tokens, -1)
    grads = wide(grads.astype(F32), right_basis)
    grads = scatter_sum(grads.reshape(nr, tokens // nr, width), "row", nr)
    grads = gather(grads, "row", nr).reshape(tokens, width) * (1.0 / tokens)

    acts = exchange_sum(exchange_sum(acts, "tok", nt), "col", nc)
    acts = [acts] + [shift(acts, "row", nr, s) for s in range(1, nr)]

    carried = share(left_basis).astype(BF16)
    ring, carried, grads = lax.optimization_barrier((ring, carried, grads))
    lefts = [left_basis.astype(BF16)]
    for s in range(1, nr):
        if s > 1:
            ring = shift(ring, "row", nr, 1)
            spectra.append(joined(ring))
        carried = shift(carried, "row", nr, 1)
        lefts.append(joined(carried))
    high, low = halves(grads)
    grads = jnp.concatenate([high, low, high], 0)

    right = right_basis.astype(BF16)
    half = block // nt

    def part(turned, values, h):
        mine = lax.dynamic_slice_in_dim(turned, h * half, half, 0)
        rotated = narrow(mine, grads, ((1,), (0,)))
        values = lax.dynamic_slice_in_dim(values, h * half, half, 0)
        scaled = (rotated / (values.astype(F32) + DAMPING)).astype(BF16)
        return narrow(lax.optimization_barrier(scaled), right, ((1,), (1,)))

    out, own, received = None, [], []
    for s in range(nr):
        if s > 1:
            received[s - 2][1], acts[s] = lax.optimization_barrier((received[s - 2][1], acts[s]))
        high, low = halves(acts[s])
        turned = jnp.concatenate([high, high, low], 0).T
        arrived = []
        for t in range(1, nt):
            arrived.append(shift(part(turned, spectra[s], (tok + t) % nt), "tok", nt, t))
        if s > 0:
            received[s - 1][0], turned = lax.optimization_barrier((received[s - 1][0], turned))
        back = part(turned, spectra[s], tok)
        for term in arrived:
            back = back + term
        sent = back.astype(BF16)
        if s + 1 < nr:
            sent, acts[s + 1] = lax.optimization_barrier((sent, acts[s + 1]))
        crossed = [
            [shift(rows, "col", nc, t) for t in range(1, nc)]
            for rows in (sent[: half // 2], sent[half // 2 :])
        ]
        own.append(back)
        received.append(crossed)
    for s in range(nr):
        back = own[s]
        for first, second in zip(*received[s]):
            back = back + jnp.concatenate([first, second], 0).astype(F32)
        back = gather(back.astype(BF16), "tok", nt).reshape(block, -1)
        term = narrow(lefts[s], back, ((1,), (0,)))
        out = term if out is None else out + term
    return out


def solution(mesh):
    sizes = dict(mesh.shape)
    return jax.shard_map(
        lambda *args: shards(sizes, *args),
        mesh=mesh,
        in_specs=(
            P(("query", "row"), ("tok", "col")),
            P(("query", "tok", "col"), "row"),
            P(("tok", "col"), "row"),
            P("row", ("tok", "col")),
            P("row", ("tok", "col")),
        ),
        out_specs=P(("query", "tok", "col"), "row"),
        check_vma=False,
    )
```

```python
import jax
import jax.numpy as jnp
from jax import lax
from jax.sharding import PartitionSpec as P

DAMPING = 0.002
F32, BF16, F16 = jnp.float32, jnp.bfloat16, jnp.float16


def shift(x, axis, n, s):
    return lax.ppermute(x, axis, [(i, (i + s) % n) for i in range(n)])


def gather(x, axis, n):
    me = lax.axis_index(axis)
    if n == 2:
        other = shift(x, axis, n, 1)
        return jnp.stack([jnp.where(me == 0, x, other), jnp.where(me == 0, other, x)])
    out = jnp.zeros((n,) + x.shape, x.dtype)
    out = lax.dynamic_update_index_in_dim(out, x, me, 0)
    for s in range(1, n):
        out = lax.dynamic_update_index_in_dim(out, shift(x, axis, n, s), (me - s) % n, 0)
    return out


def exchange_sum(x, axis, n, sent=F32):
    total = x
    for s in range(1, n):
        total = total + shift(x.astype(sent), axis, n, s).astype(F32)
    return total


def scatter_sum(x, axis, n):
    me = lax.axis_index(axis)
    total = lax.dynamic_index_in_dim(x, me, 0, keepdims=False)
    for s in range(1, n):
        part = lax.dynamic_index_in_dim(x, (me + s) % n, 0, keepdims=False)
        total = total + shift(part, axis, n, s)
    return total


def narrow(left, right, dims):
    return lax.dot_general(left, right, (dims, ((), ())), preferred_element_type=F32)


def wide(left, right):
    return jnp.dot(left, right, precision=lax.Precision.HIGH, preferred_element_type=F32)


def halves(x):
    high = lax.reduce_precision(x, 8, 7)
    return high.astype(BF16), (x - high).astype(BF16)


def shards(sizes, activations, out_grads, left_basis, right_basis, spectrum):
    nq, nt, nr, nc = (sizes[a] for a in ("query", "tok", "row", "col"))
    query, row, tok = (lax.axis_index(a) for a in ("query", "row", "tok"))
    spectrum, left_basis_turned = spectrum.T, left_basis.T
    width, block = spectrum.shape

    def share(x):
        size = x.shape[0] // nq
        return lax.dynamic_slice_in_dim(x, query * size, size, 0)

    def joined(piece):
        return gather(piece, "query", nq).reshape((-1,) + piece.shape[1:])

    spectra = [spectrum]
    ring = share(spectrum).astype(F16)
    if nr > 1:
        ring = shift(ring, "row", nr, 1)
        spectra.append(joined(ring))

    acts = gather(activations, "row", nr).reshape(-1, activations.shape[1])
    tokens = acts.shape[0]
    acts = wide(acts.astype(F32), left_basis)

    grads = gather(gather(out_grads, "col", nc), "tok", nt).reshape(tokens, -1)
    grads = wide(grads.astype(F32), right_basis)
    grads, right_basis, spectra[0], ring = lax.optimization_barrier(
        (grads, right_basis, spectra[0], ring)
    )
    for _ in range(2, min(nr, 3)):
        ring = shift(ring, "row", nr, 1)
        spectra.append(joined(ring))
    grads = scatter_sum(grads.reshape(nr, tokens // nr, width), "row", nr)
    grads = gather(grads, "row", nr).reshape(tokens, width) * (1.0 / tokens)

    acts = exchange_sum(exchange_sum(acts, "tok", nt), "col", nc)
    acts = [acts] + [shift(acts, "row", nr, s) for s in range(1, nr)]

    carried = share(left_basis_turned).astype(BF16)
    ring, carried, _ = lax.optimization_barrier((ring, carried, (grads, acts)))
    lefts = [left_basis_turned.astype(BF16)]
    for s in range(1, nr):
        if s > 2:
            ring = shift(ring, "row", nr, 1)
            spectra.append(joined(ring))
    carried, ring = lax.optimization_barrier((carried, ring))
    for s in range(1, nr):
        carried = shift(carried, "row", nr, 1)
        lefts.append(joined(carried))
    high, low = halves(grads)
    grads = jnp.concatenate([high, low, high], 0)

    right = right_basis.astype(BF16)
    outputs = right.shape[0]
    half = outputs // nt

    def rescaled(both, values):
        rotated = narrow(grads, both, ((0,), (0,)))
        scaled = (rotated / (values.astype(F32) + DAMPING)).astype(BF16)
        return lax.optimization_barrier(scaled)

    def part(scaled, h):
        return narrow(lax.dynamic_slice_in_dim(right, h * half, half, 0), scaled, ((1,), (0,)))

    def finished(s, out):
        back = own[s]
        for first, second in zip(*received[s]):
            back = back + jnp.concatenate([first, second], 0).astype(F32)
        back = gather(back.astype(BF16), "tok", nt).reshape(outputs, block)
        term = narrow(back, lefts[s], ((1,), (0,)))
        return term if out is None else out + term

    out, own, received = None, [], []
    for s in range(nr):
        if s > 1:
            received[s - 2][1], acts[s] = lax.optimization_barrier((received[s - 2][1], acts[s]))
        high, low = halves(acts[s])
        scaled = rescaled(jnp.concatenate([high, high, low], 0), spectra[s])
        arrived = []
        for t in range(1, nt):
            arrived.append(shift(part(scaled, (tok + t) % nt), "tok", nt, t))
        if s > 0:
            if s > 1:
                out = finished(s - 2, out)
                out, scaled = lax.optimization_barrier((out, scaled))
                if s == nr - 1:
                    lefts, scaled = lax.optimization_barrier((lefts, scaled))
            received[s - 1][0], scaled = lax.optimization_barrier((received[s - 1][0], scaled))
        back = part(scaled, tok)
        for term in arrived:
            back = back + term
        sent = back.astype(BF16)
        if s + 1 < nr:
            sent, acts[s + 1] = lax.optimization_barrier((sent, acts[s + 1]))
        crossed = [
            [shift(rows, "col", nc, t) for t in range(1, nc)]
            for rows in (sent[: half // 2], sent[half // 2 :])
        ]
        own.append(back)
        received.append(crossed)
    for s in range(max(nr - 2, 0), nr):
        out = finished(s, out)
    return out.T


def solution(mesh):
    sizes = dict(mesh.shape)
    return jax.shard_map(
        lambda *args: shards(sizes, *args),
        mesh=mesh,
        in_specs=(
            P(("query", "row"), ("tok", "col")),
            P(("query", "tok", "col"), "row"),
            P(("tok", "col"), "row"),
            P("row", ("tok", "col")),
            P("row", ("tok", "col")),
        ),
        out_specs=P(("query", "tok", "col"), "row"),
        check_vma=False,
    )
```
